32 devices in a mesh: groups: 2 (over x), beam: 4 (over z), ctx: 4 (over y, core).
Axes of the slice: x: 2, y: 2, z: 4, core: 2. Of those that a mesh axis runs over, the one named last changes fastest.
Arguments:
- queries: bfloat16 [8, 16384], P(('groups', 'beam'), 'ctx'), parts along dimension 0
- new_keys: bfloat16 [8, 1024], P(('groups', 'beam')), parts along dimension 0, may hold values from -16 to 16
- new_values: bfloat16 [8, 1024], P(('groups', 'beam')), parts along dimension 0, may hold values from -9 to 9
- cache_keys: bfloat16 [8, 2048, 8, 128], P(('groups', 'beam'), 'ctx'), parts along dimension 0
- cache_values: bfloat16 [8, 2048, 8, 128], P(('groups', 'beam'), 'ctx'), parts along dimension 0, may hold values from -6 to 6
- parents: int32 [8], P('groups'), parts along dimension 0, may hold values from 0 to 3
- lengths: int32 [8], P('groups'), parts along dimension 0, may hold values from 8 to 16, as said below
- out_weight: bfloat16 [16384, 16384], P('ctx', 'beam'), may hold values from -0.046875 to 0.046875
Outputs:
- projected: bfloat16 [8, 16384], P('groups', ('beam', 'ctx')), parts along dimension 0
The draws below stay inside these ranges and needn't reach their ends.
There are 2 independent parts, one for each index of `groups`. The reference program is written for one: setup_inputs(seed, part) draws one part's arguments, and reference() takes and returns one part's arrays. A program takes and returns all parts, laid end to end along the dimension named above; an argument that names none is the same for every part. Nothing has to cross between parts.
Inputs may be any that keep to these rules, and one draw needn't show every extreme that they name: `lengths`: each previous beam holds at least half of its 16 spans; in every draw some beam is full.
All inputs are finite; a program needn't handle non-finite values.
Results may differ from the reference program's by a relative error of at most 0.012.
Values may be sent and summed in bfloat16 or wider, within the bound.
A program may use at most 64 MiB of HBM per device.

```python
import math
import jax
import jax.numpy as jnp
import numpy as np
from jax import lax

D = 16384
H = 128
KVH = 8
HD = 128
SPAN = 128
BEAMS = 4
CONTEXT = 2048
SPANS = 16


def draw_queries(key, part):
    log_scale = jax.random.uniform(jax.random.fold_in(key, 4), (BEAMS, H, 1), jnp.float32, -2.302585, 2.302585)
    entries = jnp.clip(jax.random.normal(jax.random.fold_in(key, 1), (BEAMS, H, HD), jnp.float32), -4.0, 4.0)
    drawn = entries * jnp.exp(log_scale)
    return drawn.reshape(BEAMS, H * HD).astype(jnp.bfloat16)


def draw_cache_keys(key, part):
    drawn = jnp.clip(2.0 * jax.random.normal(jax.random.fold_in(key, 11), (BEAMS, CONTEXT, KVH, HD), jnp.float32), -12.0, 12.0)
    return drawn.astype(jnp.bfloat16)


def draw_lengths(key, part):
    drawn = jax.random.randint(jax.random.fold_in(key, 5), (BEAMS,), SPANS // 2, SPANS + 1)
    fullest = jax.random.randint(jax.random.fold_in(key, 6), (), 0, BEAMS)
    return jnp.where(jnp.arange(BEAMS, dtype=jnp.int32) == fullest, SPANS, drawn).astype(jnp.int32)


def with_ends(entries, key, smallest, high):
    longest = entries.shape.index(max(entries.shape))
    spots = []
    for shift in (0, 1):
        where = [jax.random.randint(jax.random.fold_in(key, axis), (), 0, length) for axis, length in enumerate(entries.shape)]
        where[longest] = (where[longest] + shift) % entries.shape[longest]
        spots.append(tuple(where))
    return entries.at[spots[0]].set(smallest).at[spots[1]].set(high)


def block_scale(own_key, extent, shards, least, high):
    level, own = 1.0, jax.random.fold_in(own_key, 6)
    for dim, shards_of in shards:
        steps = jnp.exp(jax.random.uniform(jax.random.fold_in(own, dim), (shards_of,), jnp.float32, least / len(shards), high / len(shards)))
        level = level * jnp.repeat(steps, extent[dim] // shards_of).reshape([-1 if axis == dim else 1 for axis in range(len(extent))])
    return level


def cumulative_ranks(amount, lean):
    weights = [(1 << 20) // math.isqrt(grade ** lean) + 1 for grade in range(1, amount + 1)]
    deviation = 1 + sum(weights) // (1 << 30)
    return np.cumsum(np.array([max(1, weight // deviation) for weight in weights]))


def skewed_ids(key, extent, amount, lean):
    grid = cumulative_ranks(amount, lean)
    ticket = jax.random.randint(jax.random.fold_in(key, 1), extent, 0, int(grid[amount - 1]))
    standing = jnp.searchsorted(jnp.asarray(grid, jnp.int32), ticket, side="right")
    return jax.random.permutation(jax.random.fold_in(key, 2), amount)[standing].astype(jnp.int32)


def gaussian(own_key, dims, spread, limit, split=(), kind=jnp.bfloat16):
    factor_of = block_scale(own_key, dims, split, -0.22, 0.18) if split else 1.0
    values = jax.random.normal(own_key, dims, jnp.float32) * spread * factor_of
    return jnp.minimum(jnp.maximum(values, -limit), limit).astype(kind)


def setup_inputs(seed: int = 0, part: int = 0) -> dict:
    key_list = jax.random.split(jax.random.key(seed), 9)
    own_keys = jax.random.split(jax.random.fold_in(key_list[8], part), 9)
    return {
        "queries": draw_queries(jax.random.fold_in(jax.random.fold_in(key_list[8], part), 71), part),
        "new_keys": gaussian(own_keys[1], (BEAMS, KVH * HD), 4.0, 16.0, ((0, 4),)),
        "new_values": gaussian(own_keys[2], (BEAMS, KVH * HD), 1.5, 9.0, ((0, 4),)),
        "cache_keys": draw_cache_keys(jax.random.fold_in(jax.random.fold_in(key_list[8], part), 71), part),
        "cache_values": gaussian(own_keys[4], (BEAMS, CONTEXT, KVH, HD), 1.0, 6.0, ((0, 4), (1, 4))),
        "parents": with_ends(skewed_ids(own_keys[5], (BEAMS,), BEAMS, 2), jax.random.fold_in(own_keys[5], 3), 0, BEAMS - 1).astype(jnp.int32),
        "lengths": draw_lengths(jax.random.fold_in(jax.random.fold_in(key_list[8], part), 71), part),
        "out_weight": gaussian(key_list[7], (H * HD, D), (H * HD) ** -0.5, 0.046875, ((0, 4), (1, 4))),
    }


MASKED = -1e+30

def attend_child(query, new_key, new_value, parent_keys, parent_values, length):
    group_size = H // KVH
    scale = 1.0 / math.sqrt(HD)
    grouped = query.astype(jnp.float32).reshape(KVH, group_size, HD)
    scores = jnp.einsum('kgd,tkd->kgt', grouped, parent_keys.astype(jnp.float32)) * scale
    usable = jnp.arange(CONTEXT, dtype=jnp.int32) < length * SPAN
    scores = jnp.where(usable[None, None, :], scores, MASKED)
    own_score = jnp.einsum('kgd,kd->kg', grouped, new_key.astype(jnp.float32).reshape(KVH, HD)) * scale
    peak = jnp.maximum(lax.optimization_barrier(jnp.max(scores, axis=-1)), own_score)
    weights = jnp.where(usable[None, None, :], jnp.exp(scores - peak[..., None]), 0.0)
    own_weight = jnp.exp(own_score - peak)
    weight_sum = lax.optimization_barrier(jnp.sum(weights, axis=-1)) + own_weight
    rounded = lax.optimization_barrier(weights.astype(jnp.bfloat16)).astype(jnp.float32)
    own_rounded = lax.optimization_barrier(own_weight.astype(jnp.bfloat16)).astype(jnp.float32)
    blended = jnp.einsum('kgt,tkd->kgd', rounded, parent_values.astype(jnp.float32))
    blended = blended + own_rounded[..., None] * new_value.astype(jnp.float32).reshape(KVH, 1, HD)
    return (blended / weight_sum[..., None]).reshape(H * HD).astype(jnp.bfloat16)

def reference(queries, new_keys, new_values, cache_keys, cache_values, parents, lengths, out_weight):

    def per_child(child):
        parent = parents[child]
        return attend_child(queries[child], new_keys[child], new_values[child], cache_keys[parent], cache_values[parent], lengths[parent])
    attended = lax.map(per_child, jnp.arange(BEAMS, dtype=jnp.int32))
    return jnp.dot(attended, out_weight, preferred_element_type=jnp.float32).astype(jnp.bfloat16)
```

```python
import functools
import math

import jax
import jax.numpy as jnp
from jax import lax
from jax.experimental import pallas as pl
from jax.experimental.pallas import tpu as pltpu
from jax.sharding import PartitionSpec as P

H = 128
KVH = 8
HD = 128
SPAN = 128
GROUP = H // KVH
MASKED = -1e30
LANES = 128
MESH = pl.DeviceIdType.MESH
F32 = jnp.float32
BF16 = jnp.bfloat16


def split3(x):
    hi = x.astype(BF16).astype(F32)
    mid = (x - hi).astype(BF16).astype(F32)
    return hi, mid, x - hi - mid


def kernel(
    nb, nc, hs, rows_total, tokens,
    q_hbm, nk_hbm, nv_hbm, ck_hbm, cv_hbm, par_hbm, len_hbm, w_hbm,
    out_ref,
    w_vm, ck_vm, cv_vm, k32, v32, kh, vh,
    q_in, nk_in, nv_in, par_sm, len_sm,
    q_rows, q_buf, n_buf, d_send, d_recv, e_buf, a_rows, g_send, g_recv,
    in_sem, w_sem, qs_sem, qr_sem, ns_sem, nr_sem, ds_sem, dr_sem,
    es_sem, er_sem, gs_sem, gr_sem,
):
    g = lax.axis_index("groups")
    p = lax.axis_index("beam")
    c = lax.axis_index("ctx")
    rp = max(hs, GROUP)
    units = rp // GROUP
    ur = nb * GROUP
    quarter = w_vm.shape[2]

    def dev(b, s):
        return (g, b, s)

    def cmod(k):
        return lax.rem(c + k, nc)

    def pmod(j):
        return lax.rem(p + j, nb)

    loads = []
    for i, (src, dst) in enumerate(
        (
            (q_hbm, q_in), (nk_hbm, nk_in), (nv_hbm, nv_in),
            (par_hbm, par_sm), (len_hbm, len_sm),
            (ck_hbm.at[0], ck_vm), (cv_hbm.at[0], cv_vm),
        )
    ):
        load = pltpu.make_async_copy(src, dst, in_sem.at[i])
        load.start()
        loads.append(load)

    def w_load(k):
        s = cmod(k)
        return pltpu.make_async_copy(
            w_hbm.at[:, pl.ds(pl.multiple_of(s * quarter, quarter), quarter)],
            w_vm.at[s],
            w_sem.at[k],
        )

    order = [k for k in range(1, nc)] + [0]
    for k in order:
        w_load(k).start()

    barrier = pltpu.get_barrier_semaphore()

    def greet(i, carry):
        b = pmod(i // nc)
        s = cmod(lax.rem(i, nc))
        pl.semaphore_signal(barrier, inc=1, device_id=dev(b, s), device_id_type=MESH)
        return carry

    lax.fori_loop(1, nb * nc, greet, 0)

    for i in range(3):
        loads[i].wait()
    q_rows[...] = jnp.zeros_like(q_rows)
    q_flat = q_in[...].astype(F32)
    for h in range(hs):
        q_rows[h : h + 1, :] = q_flat[:, h * HD : (h + 1) * HD]
    q_buf[c, p] = q_rows[...].astype(BF16)
    kv0 = (c * hs) // GROUP
    row16 = lax.broadcasted_iota(jnp.int32, (16, HD), 0)
    staged = jnp.zeros((16, HD), F32)
    for u in range(units):
        lane0 = pl.multiple_of((kv0 + u) * HD, HD)
        staged = jnp.where(row16 == u, nk_in[:, pl.ds(lane0, HD)].astype(F32), staged)
        staged = jnp.where(row16 == 8 + u, nv_in[:, pl.ds(lane0, HD)].astype(F32), staged)
    n_buf[p] = staged.astype(BF16)

    pl.semaphore_wait(barrier, nb * nc - 1)

    def q_copy(j, k):
        return pltpu.make_async_remote_copy(
            src_ref=q_buf.at[c, p],
            dst_ref=q_buf.at[c, p],
            send_sem=qs_sem.at[j, k],
            recv_sem=qr_sem.at[c, p],
            device_id=dev(pmod(j), cmod(k)),
            device_id_type=MESH,
        )

    def n_copy(j):
        return pltpu.make_async_remote_copy(
            src_ref=n_buf.at[p],
            dst_ref=n_buf.at[p],
            send_sem=ns_sem.at[j],
            recv_sem=nr_sem.at[p],
            device_id=dev(pmod(j), c),
            device_id_type=MESH,
        )

    def q_arrival(b, s):
        return pltpu.make_async_remote_copy(
            src_ref=q_buf.at[s, b],
            dst_ref=q_buf.at[s, b],
            send_sem=qs_sem.at[0, 0],
            recv_sem=qr_sem.at[s, b],
            device_id=dev(pmod(1), c),
            device_id_type=MESH,
        )

    for k in range(nc - 1, -1, -1):
        for j in range(nb - 1, -1, -1):
            if j or k:
                q_copy(j, k).start()
    for j in range(nb - 1, 0, -1):
        n_copy(j).start()

    loads[5].wait()
    step = 64

    def widen(src, dst):
        def body(i, carry):
            t0 = pl.multiple_of(i * step, step)
            block = src[pl.ds(t0, step)].astype(F32)
            dst[pl.ds(pl.multiple_of(t0 * KVH, step * KVH), step * KVH), :] = block.reshape(
                step * KVH, HD
            )
            return carry

        lax.fori_loop(0, tokens // step, body, 0)

    widen(ck_vm, k32)
    for kv in range(KVH):
        kh[kv] = k32[pl.ds(kv, tokens, stride=KVH), :].astype(BF16)
    loads[6].wait()
    widen(cv_vm, v32)
    for kv in range(KVH):
        vh[kv] = v32[pl.ds(kv, tokens, stride=KVH), :].astype(BF16)
    loads[3].wait()
    loads[4].wait()
    limit = len_sm[p] * SPAN
    position = c * tokens + lax.broadcasted_iota(jnp.int32, (ur, tokens), 1)
    usable = position < limit
    scale = 1.0 / math.sqrt(HD)
    lane_u = lax.broadcasted_iota(jnp.int32, (ur, LANES), 1)
    row_u = lax.broadcasted_iota(jnp.int32, (ur, LANES), 0)
    row16 = lax.broadcasted_iota(jnp.int32, (16, LANES), 0)

    def to_lanes(column, u):
        return jnp.sum(jnp.where(lane_u == row_u + u * ur, column, 0.0), axis=0, keepdims=True)

    def attend(s):
        kv_base = (s * hs) // GROUP
        peak_row = jnp.zeros((1, LANES), F32)
        sum_row = jnp.zeros((1, LANES), F32)
        for u in range(units):
            q = jnp.concatenate(
                [q_buf[s, b, u * GROUP : (u + 1) * GROUP, :] for b in range(nb)], axis=0
            )
            scores = lax.dot_general(
                q, kh[kv_base + u], (((1,), (1,)), ((), ())), preferred_element_type=F32
            )
            scores = jnp.where(usable, scores * scale, MASKED)
            peak = jnp.max(scores, axis=1, keepdims=True)
            weights = jnp.where(usable, jnp.exp(scores - peak), 0.0)
            total = jnp.sum(weights, axis=1, keepdims=True)
            blended = jnp.dot(weights.astype(BF16), vh[kv_base + u], preferred_element_type=F32)
            d_send[s, u * ur : (u + 1) * ur, :] = blended.astype(BF16)
            peak_row = peak_row + to_lanes(peak, u)
            sum_row = sum_row + to_lanes(total, u)
        stats = jnp.zeros((16, LANES), F32)
        for i, piece in enumerate(split3(peak_row) + split3(sum_row)):
            stats = jnp.where(row16 == i, piece, stats)
        d_send[s, units * ur : units * ur + 16, :] = stats.astype(BF16)

    def d_copy(k):
        return pltpu.make_async_remote_copy(
            src_ref=d_send.at[cmod(k)],
            dst_ref=d_recv.at[c],
            send_sem=ds_sem.at[k],
            recv_sem=dr_sem.at[c],
            device_id=dev(p, cmod(k)),
            device_id_type=MESH,
        )

    def d_arrival(s):
        return pltpu.make_async_remote_copy(
            src_ref=d_recv.at[s],
            dst_ref=d_recv.at[s],
            send_sem=ds_sem.at[0],
            recv_sem=dr_sem.at[s],
            device_id=dev(p, cmod(1)),
            device_id_type=MESH,
        )

    for k in order:
        s = cmod(k)
        for j in range(nb):
            if j or k:
                q_arrival(pmod(j), s).wait_recv()
        attend(s)
        if k:
            d_copy(k).start()

    for j in range(1, nb):
        pltpu.make_async_remote_copy(
            src_ref=n_buf.at[pmod(j)],
            dst_ref=n_buf.at[pmod(j)],
            send_sem=ns_sem.at[0],
            recv_sem=nr_sem.at[pmod(j)],
            device_id=dev(pmod(j), c),
            device_id_type=MESH,
        ).wait_recv()
    own_row = jnp.zeros((1, LANES), F32)
    own_values = []
    for u in range(units):
        own_scores = []
        for b in range(nb):
            fresh = n_buf[b].astype(F32)
            q = q_buf[c, b, u * GROUP : (u + 1) * GROUP, :].astype(F32)
            own_scores.append(jnp.sum(q * fresh[u : u + 1], axis=1, keepdims=True))
            own_values.append(jnp.broadcast_to(fresh[8 + u : 9 + u], (GROUP, HD)))
        own_row = own_row + to_lanes(
            jnp.broadcast_to(jnp.concatenate(own_scores, axis=0), (ur, LANES)), u
        )
    own_row = own_row * scale
    own_value = jnp.concatenate(own_values, axis=0)

    for k in range(1, nc):
        d_arrival(cmod(k)).wait_recv()
    rows = units * ur
    states = []
    for k in range(nc):
        ref = d_send if k == 0 else d_recv
        s = cmod(k)
        stats = ref[s, rows : rows + 16, :].astype(F32)
        states.append(
            (
                ref, s,
                stats[0:1] + stats[1:2] + stats[2:3],
                stats[3:4] + stats[4:5] + stats[5:6],
            )
        )
    top = own_row
    for _, _, peak, _ in states:
        top = jnp.maximum(top, peak)
    own_scale = jnp.exp(own_row - top)
    total = own_scale
    scales = []
    for _, _, peak, weight_sum in states:
        factor = jnp.exp(peak - top)
        scales.append(factor)
        total = total + weight_sum * factor
    inverse = 1.0 / total
    lane_r = lax.broadcasted_iota(jnp.int32, (rows, LANES), 1)
    row_r = lax.broadcasted_iota(jnp.int32, (rows, LANES), 0)
    diagonal = lane_r == row_r

    def to_rows(lanes):
        return jnp.sum(jnp.where(diagonal, lanes, 0.0), axis=1, keepdims=True)

    result = own_value * to_rows(own_scale * inverse)
    for (ref, s, _, _), factor in zip(states, scales):
        result = result + ref[s, 0:rows, :].astype(F32) * to_rows(factor * inverse)
    e_buf[p] = result.astype(BF16)

    def e_copy(j):
        return pltpu.make_async_remote_copy(
            src_ref=e_buf.at[p],
            dst_ref=e_buf.at[p],
            send_sem=es_sem.at[j],
            recv_sem=er_sem.at[p],
            device_id=dev(pmod(j), c),
            device_id_type=MESH,
        )

    for j in range(nb - 1, 0, -1):
        e_copy(j).start()
    for j in range(1, nb):
        pltpu.make_async_remote_copy(
            src_ref=e_buf.at[pmod(j)],
            dst_ref=e_buf.at[pmod(j)],
            send_sem=es_sem.at[0],
            recv_sem=er_sem.at[pmod(j)],
            device_id=dev(pmod(j), c),
            device_id_type=MESH,
        ).wait_recv()
    for b in range(nb):
        parent = par_sm[b]
        for u in range(units):
            r0 = u * ur + b * GROUP
            a_rows[r0 : r0 + GROUP, :] = e_buf[parent, r0 : r0 + GROUP, :].astype(F32)
    heads = []
    for h in range(hs):
        r0 = (h // GROUP) * ur + h % GROUP
        heads.append(a_rows[pl.ds(r0, nb, stride=GROUP), :])
    attended = jnp.concatenate(heads, axis=1).astype(BF16)

    def g_copy(k):
        return pltpu.make_async_remote_copy(
            src_ref=g_send.at[cmod(k)],
            dst_ref=g_recv.at[c],
            send_sem=gs_sem.at[k],
            recv_sem=gr_sem.at[c],
            device_id=dev(p, cmod(k)),
            device_id_type=MESH,
        )

    chunk = min(512, quarter)
    for k in order:
        s = cmod(k)
        w_load(k).wait()

        def multiply(i, carry):
            n0 = pl.multiple_of(i * chunk, chunk)
            g_send[s, :, pl.ds(n0, chunk)] = jnp.dot(
                attended, w_vm[s, :, pl.ds(n0, chunk)], preferred_element_type=F32
            )
            return carry

        lax.fori_loop(0, quarter // chunk, multiply, 0)
        if k:
            g_copy(k).start()
    total_out = g_send[c]
    for k in range(1, nc):
        s = cmod(k)
        pltpu.make_async_remote_copy(
            src_ref=g_recv.at[s],
            dst_ref=g_recv.at[s],
            send_sem=gs_sem.at[0],
            recv_sem=gr_sem.at[s],
            device_id=dev(p, cmod(1)),
            device_id_type=MESH,
        ).wait_recv()
        total_out = total_out + g_recv[s]
    out_ref[...] = total_out.astype(BF16)

    for k in range(nc):
        for j in range(nb):
            if j or k:
                q_copy(j, k).wait_send()
    for j in range(1, nb):
        n_copy(j).wait_send()
        e_copy(j).wait_send()
    for k in range(1, nc):
        d_copy(k).wait_send()
        g_copy(k).wait_send()


def per_device(nb, nc, queries, new_keys, new_values, cache_keys, cache_values, parents, lengths, out_weight):
    hs = queries.shape[1] // HD
    tokens = cache_keys.shape[1]
    rp = max(hs, GROUP)
    rows = (rp // GROUP) * nb * GROUP
    depth, columns = out_weight.shape
    quarter = columns // nc
    dma = pltpu.SemaphoreType.DMA
    return pl.pallas_call(
        functools.partial(kernel, nb, nc, hs, rows, tokens),
        out_shape=jax.ShapeDtypeStruct((nb, quarter), BF16),
        in_specs=[pl.BlockSpec(memory_space=pl.ANY)] * 8,
        out_specs=pl.BlockSpec(memory_space=pltpu.VMEM),
        scratch_shapes=[
            pltpu.VMEM((nc, depth, quarter), BF16),
            pltpu.VMEM((tokens, KVH, HD), BF16),
            pltpu.VMEM((tokens, KVH, HD), BF16),
            pltpu.VMEM((tokens * KVH, HD), F32),
            pltpu.VMEM((tokens * KVH, HD), F32),
            pltpu.VMEM((KVH, tokens, HD), BF16),
            pltpu.VMEM((KVH, tokens, HD), BF16),
            pltpu.VMEM(queries.shape, BF16),
            pltpu.VMEM(new_keys.shape, BF16),
            pltpu.VMEM(new_values.shape, BF16),
            pltpu.SMEM(parents.shape, jnp.int32),
            pltpu.SMEM(lengths.shape, jnp.int32),
            pltpu.VMEM((rp, HD), F32),
            pltpu.VMEM((nc, nb, rp, HD), BF16),
            pltpu.VMEM((nb, 16, HD), BF16),
            pltpu.VMEM((nc, rows + 16, HD), BF16),
            pltpu.VMEM((nc, rows + 16, HD), BF16),
            pltpu.VMEM((nb, rows, HD), BF16),
            pltpu.VMEM((rows, HD), F32),
            pltpu.VMEM((nc, nb, quarter), F32),
            pltpu.VMEM((nc, nb, quarter), F32),
            dma((7,)),
            dma((nc,)),
            dma((nb, nc)),
            dma((nc, nb)),
            dma((nb,)),
            dma((nb,)),
            dma((nc,)),
            dma((nc,)),
            dma((nb,)),
            dma((nb,)),
            dma((nc,)),
            dma((nc,)),
        ],
        compiler_params=pltpu.CompilerParams(
            collective_id=0, has_side_effects=True, vmem_limit_bytes=60 * 1024 * 1024
        ),
    )(queries, new_keys, new_values, cache_keys, cache_values, parents, lengths, out_weight)


def solution(mesh):
    placed = (
        P(("groups", "beam"), "ctx"),
        P(("groups", "beam"), None),
        P(("groups", "beam"), None),
        P(("groups", "beam"), "ctx", None, None),
        P(("groups", "beam"), "ctx", None, None),
        P("groups"),
        P("groups"),
        P("ctx", "beam"),
    )
    return jax.shard_map(
        functools.partial(per_device, mesh.shape["beam"], mesh.shape["ctx"]),
        mesh=mesh,
        in_specs=placed,
        out_specs=P("groups", ("beam", "ctx")),
        check_vma=False,
    )
```

```python
import functools
import math

import jax
import jax.numpy as jnp
from jax import lax
from jax.experimental import pallas as pl
from jax.experimental.pallas import tpu as pltpu
from jax.sharding import PartitionSpec as P

H = 128
KVH = 8
HD = 128
SPAN = 128
GROUP = H // KVH
LOWEST = -3.0e38
LANES = 128
MESH = pl.DeviceIdType.MESH
F32 = jnp.float32
BF16 = jnp.bfloat16


def split3(x):
    hi = x.astype(BF16).astype(F32)
    mid = (x - hi).astype(BF16).astype(F32)
    return hi, mid, x - hi - mid


def kernel(
    nb, nc, hs, tokens,
    q_hbm, nk_hbm, nv_hbm, ck_hbm, cv_hbm, par_hbm, len_hbm, w_hbm,
    out_ref,
    w_vm, ck_vm, cv_vm, k32, v32, kh, vh,
    q_in, nk_in, nv_in, par_sm, len_sm,
    q_rows, q_buf, n_buf, d_send, d_recv, e_buf, a_rows, g_send, g_recv,
    in_sem, w_sem, qs_sem, qr_sem, ns_sem, nr_sem, ds_sem, dr_sem,
    es_sem, er_sem, gs_sem, gr_sem,
):
    g = lax.axis_index("groups")
    p = lax.axis_index("beam")
    c = lax.axis_index("ctx")
    rp = max(hs, GROUP)
    units = rp // GROUP
    ur = nb * GROUP
    quarter = w_vm.shape[2]

    def dev(b, s):
        return (g, b, s)

    def cmod(k):
        return lax.rem(c + k, nc)

    def pmod(j):
        return lax.rem(p + j, nb)

    loads = []
    for i, (src, dst) in enumerate(
        (
            (q_hbm, q_in), (nk_hbm, nk_in), (nv_hbm, nv_in),
            (par_hbm, par_sm), (len_hbm, len_sm),
            (ck_hbm.at[0], ck_vm), (cv_hbm.at[0], cv_vm),
        )
    ):
        load = pltpu.make_async_copy(src, dst, in_sem.at[i])
        load.start()
        loads.append(load)

    part = w_vm.shape[1] // units

    def w_load(u, k):
        s = cmod(k)
        return pltpu.make_async_copy(
            w_hbm.at[
                u * part : (u + 1) * part,
                pl.ds(pl.multiple_of(s * quarter, quarter), quarter),
            ],
            w_vm.at[s, u * part : (u + 1) * part],
            w_sem.at[u, k],
        )

    order = [k for k in range(1, nc)] + [0]
    for u in range(units):
        for k in order:
            w_load(u, k).start()

    barrier = pltpu.get_barrier_semaphore()

    def greet(i, carry):
        b = pmod(i // nc)
        s = cmod(lax.rem(i, nc))
        pl.semaphore_signal(barrier, inc=1, device_id=dev(b, s), device_id_type=MESH)
        return carry

    lax.fori_loop(1, nb * nc, greet, 0)

    for i in range(3):
        loads[i].wait()
    q_rows[...] = jnp.zeros_like(q_rows)
    q_flat = q_in[...].astype(F32)
    for h in range(hs):
        q_rows[h : h + 1, :] = q_flat[:, h * HD : (h + 1) * HD]
    q_buf[c, p] = q_rows[...].astype(BF16)
    kv0 = (c * hs) // GROUP
    row16 = lax.broadcasted_iota(jnp.int32, (16, HD), 0)
    staged = jnp.zeros((16, HD), F32)
    for u in range(units):
        lane0 = pl.multiple_of((kv0 + u) * HD, HD)
        staged = jnp.where(row16 == u, nk_in[:, pl.ds(lane0, HD)].astype(F32), staged)
        staged = jnp.where(row16 == 8 + u, nv_in[:, pl.ds(lane0, HD)].astype(F32), staged)
    n_buf[p] = staged.astype(BF16)

    pl.semaphore_wait(barrier, nb * nc - 1)

    def q_copy(j, k):
        return pltpu.make_async_remote_copy(
            src_ref=q_buf.at[c, p],
            dst_ref=q_buf.at[c, p],
            send_sem=qs_sem.at[j, k],
            recv_sem=qr_sem.at[c, p],
            device_id=dev(pmod(j), cmod(k)),
            device_id_type=MESH,
        )

    def n_copy(j):
        return pltpu.make_async_remote_copy(
            src_ref=n_buf.at[p],
            dst_ref=n_buf.at[p],
            send_sem=ns_sem.at[j],
            recv_sem=nr_sem.at[p],
            device_id=dev(pmod(j), c),
            device_id_type=MESH,
        )

    def q_arrival(b, s):
        return pltpu.make_async_remote_copy(
            src_ref=q_buf.at[s, b],
            dst_ref=q_buf.at[s, b],
            send_sem=qs_sem.at[0, 0],
            recv_sem=qr_sem.at[s, b],
            device_id=dev(pmod(1), c),
            device_id_type=MESH,
        )

    for k in range(nc - 1, -1, -1):
        for j in range(nb - 1, -1, -1):
            if j or k:
                q_copy(j, k).start()
    for j in range(nb - 1, 0, -1):
        n_copy(j).start()

    loads[5].wait()
    step = 64

    def widen(src, dst):
        def body(i, carry):
            t0 = pl.multiple_of(i * step, step)
            block = src[pl.ds(t0, step)].astype(F32)
            dst[pl.ds(pl.multiple_of(t0 * KVH, step * KVH), step * KVH), :] = block.reshape(
                step * KVH, HD
            )
            return carry

        lax.fori_loop(0, tokens // step, body, 0)

    def extract(u):
        for kv in range(u, KVH, units):
            kh[kv] = k32[pl.ds(kv, tokens, stride=KVH), :].astype(BF16)
        for kv in range(u, KVH, units):
            vh[kv] = v32[pl.ds(kv, tokens, stride=KVH), :].astype(BF16)

    widen(ck_vm, k32)
    loads[6].wait()
    widen(cv_vm, v32)
    extract(0)
    loads[3].wait()
    loads[4].wait()
    limit = len_sm[p] * SPAN
    position = c * tokens + lax.broadcasted_iota(jnp.int32, (ur, tokens), 1)
    usable = position < limit
    scale = 1.0 / math.sqrt(HD)
    lane_u = lax.broadcasted_iota(jnp.int32, (ur, LANES), 1)
    row_u = lax.broadcasted_iota(jnp.int32, (ur, LANES), 0)
    row16 = lax.broadcasted_iota(jnp.int32, (16, LANES), 0)

    def to_lanes(column):
        return jnp.sum(jnp.where(lane_u == row_u, column, 0.0), axis=0, keepdims=True)

    def attend(s, u):
        kv = (s * hs) // GROUP + u
        q = jnp.concatenate(
            [q_buf[s, b, u * GROUP : (u + 1) * GROUP, :] for b in range(nb)], axis=0
        )
        scores = lax.dot_general(
            q, kh[kv], (((1,), (1,)), ((), ())), preferred_element_type=F32
        )
        scores = jnp.where(usable, scores * scale, -jnp.inf)
        peak = jnp.maximum(jnp.max(scores, axis=1, keepdims=True), LOWEST)
        weights = jnp.exp(scores - peak)
        total = jnp.sum(weights, axis=1, keepdims=True)
        blended = jnp.dot(weights.astype(BF16), vh[kv], preferred_element_type=F32)
        d_send[u, s, 0:ur, :] = blended.astype(BF16)
        stats = jnp.zeros((16, LANES), F32)
        for i, piece in enumerate(split3(to_lanes(peak)) + split3(to_lanes(total))):
            stats = jnp.where(row16 == i, piece, stats)
        d_send[u, s, ur : ur + 16, :] = stats.astype(BF16)

    def d_copy(u, k):
        return pltpu.make_async_remote_copy(
            src_ref=d_send.at[u, cmod(k)],
            dst_ref=d_recv.at[u, c],
            send_sem=ds_sem.at[u, k],
            recv_sem=dr_sem.at[u, c],
            device_id=dev(p, cmod(k)),
            device_id_type=MESH,
        )

    def d_arrival(u, s):
        return pltpu.make_async_remote_copy(
            src_ref=d_recv.at[u, s],
            dst_ref=d_recv.at[u, s],
            send_sem=ds_sem.at[u, 0],
            recv_sem=dr_sem.at[u, s],
            device_id=dev(p, cmod(1)),
            device_id_type=MESH,
        )

    for k in order:
        for j in range(nb):
            if j or k:
                q_arrival(pmod(j), cmod(k)).wait_recv()
    for u in range(units):
        if u:
            extract(u)
        for k in order:
            attend(cmod(k), u)
        for k in range(1, nc):
            d_copy(u, k).start()

    for j in range(1, nb):
        pltpu.make_async_remote_copy(
            src_ref=n_buf.at[pmod(j)],
            dst_ref=n_buf.at[pmod(j)],
            send_sem=ns_sem.at[0],
            recv_sem=nr_sem.at[pmod(j)],
            device_id=dev(pmod(j), c),
            device_id_type=MESH,
        ).wait_recv()
    own_rows = []
    own_values = []
    for u in range(units):
        own_scores = []
        unit_values = []
        for b in range(nb):
            fresh = n_buf[b].astype(F32)
            q = q_buf[c, b, u * GROUP : (u + 1) * GROUP, :].astype(F32)
            own_scores.append(jnp.sum(q * fresh[u : u + 1], axis=1, keepdims=True))
            unit_values.append(jnp.broadcast_to(fresh[8 + u : 9 + u], (GROUP, HD)))
        own_rows.append(to_lanes(jnp.concatenate(own_scores, axis=0)) * scale)
        own_values.append(jnp.concatenate(unit_values, axis=0))

    def to_rows(lanes):
        return jnp.sum(jnp.where(lane_u == row_u, lanes, 0.0), axis=1, keepdims=True)

    def combine(u):
        for k in range(1, nc):
            d_arrival(u, cmod(k)).wait_recv()
        states = []
        for k in range(nc):
            ref = d_send if k == 0 else d_recv
            s = cmod(k)
            stats = ref[u, s, ur : ur + 16, :].astype(F32)
            states.append(
                (
                    ref[u, s, 0:ur, :].astype(F32),
                    stats[0:1] + stats[1:2] + stats[2:3],
                    stats[3:4] + stats[4:5] + stats[5:6],
                )
            )
        top = own_rows[u]
        for _, peak, _ in states:
            top = jnp.maximum(top, peak)
        own_scale = jnp.exp(own_rows[u] - top)
        total = own_scale
        scales = []
        for _, peak, weight_sum in states:
            factor = jnp.exp(peak - top)
            scales.append(factor)
            total = total + weight_sum * factor
        inverse = 1.0 / total
        result = own_values[u] * to_rows(own_scale * inverse)
        for (blended, _, _), factor in zip(states, scales):
            result = result + blended * to_rows(factor * inverse)
        e_buf[u, p] = result.astype(BF16)

    def e_copy(u, j):
        return pltpu.make_async_remote_copy(
            src_ref=e_buf.at[u, p],
            dst_ref=e_buf.at[u, p],
            send_sem=es_sem.at[u, j],
            recv_sem=er_sem.at[u, p],
            device_id=dev(pmod(j), c),
            device_id_type=MESH,
        )

    def e_arrival(u, j):
        return pltpu.make_async_remote_copy(
            src_ref=e_buf.at[u, pmod(j)],
            dst_ref=e_buf.at[u, pmod(j)],
            send_sem=es_sem.at[u, 0],
            recv_sem=er_sem.at[u, pmod(j)],
            device_id=dev(pmod(j), c),
            device_id_type=MESH,
        )

    for u in range(units):
        combine(u)
        for j in range(nb - 1, 0, -1):
            e_copy(u, j).start()

    unit_heads = hs // units

    def gather_attended(u):
        for j in range(1, nb):
            e_arrival(u, j).wait_recv()
        for b in range(nb):
            r0 = b * GROUP
            chosen = e_buf[u, 0, r0 : r0 + GROUP, :].astype(F32)
            for j in range(1, nb):
                other = e_buf[u, j, r0 : r0 + GROUP, :].astype(F32)
                chosen = jnp.where(par_sm[b] == j, other, chosen)
            a_rows[u, r0 : r0 + GROUP, :] = chosen
        heads = [a_rows[u, pl.ds(h, nb, stride=GROUP), :] for h in range(unit_heads)]
        return jnp.concatenate(heads, axis=1).astype(BF16)

    def g_copy(k):
        return pltpu.make_async_remote_copy(
            src_ref=g_send.at[cmod(k)],
            dst_ref=g_recv.at[c],
            send_sem=gs_sem.at[k],
            recv_sem=gr_sem.at[c],
            device_id=dev(p, cmod(k)),
            device_id_type=MESH,
        )

    chunk = min(512, quarter)
    for u in range(units):
        attended = gather_attended(u)
        for k in order:
            s = cmod(k)
            w_load(u, k).wait()

            def multiply(i, carry):
                n0 = pl.multiple_of(i * chunk, chunk)
                product = jnp.dot(
                    attended,
                    w_vm[s, u * part : (u + 1) * part, pl.ds(n0, chunk)],
                    preferred_element_type=F32,
                )
                if u:
                    product = product + g_send[s, :, pl.ds(n0, chunk)]
                g_send[s, :, pl.ds(n0, chunk)] = product
                return carry

            lax.fori_loop(0, quarter // chunk, multiply, 0)
            if k and u == units - 1:
                g_copy(k).start()
    total_out = g_send[c]
    for k in range(1, nc):
        s = cmod(k)
        pltpu.make_async_remote_copy(
            src_ref=g_recv.at[s],
            dst_ref=g_recv.at[s],
            send_sem=gs_sem.at[0],
            recv_sem=gr_sem.at[s],
            device_id=dev(p, cmod(1)),
            device_id_type=MESH,
        ).wait_recv()
        total_out = total_out + g_recv[s]
    out_ref[...] = total_out.astype(BF16)

    for k in range(nc):
        for j in range(nb):
            if j or k:
                q_copy(j, k).wait_send()
    for j in range(1, nb):
        n_copy(j).wait_send()
    for u in range(units):
        for j in range(1, nb):
            e_copy(u, j).wait_send()
        for k in range(1, nc):
            d_copy(u, k).wait_send()
    for k in range(1, nc):
        g_copy(k).wait_send()


def per_device(nb, nc, queries, new_keys, new_values, cache_keys, cache_values, parents, lengths, out_weight):
    hs = queries.shape[1] // HD
    tokens = cache_keys.shape[1]
    rp = max(hs, GROUP)
    units = rp // GROUP
    ur = nb * GROUP
    depth, columns = out_weight.shape
    quarter = columns // nc
    dma = pltpu.SemaphoreType.DMA
    return pl.pallas_call(
        functools.partial(kernel, nb, nc, hs, tokens),
        out_shape=pltpu.VMEM((nb, quarter), BF16),
        in_specs=[pl.BlockSpec(memory_space=pltpu.HBM)] * 8,
        out_specs=pl.BlockSpec(memory_space=pltpu.VMEM),
        scratch_shapes=[
            pltpu.VMEM((nc, depth, quarter), BF16),
            pltpu.VMEM((tokens, KVH, HD), BF16),
            pltpu.VMEM((tokens, KVH, HD), BF16),
            pltpu.VMEM((tokens * KVH, HD), F32),
            pltpu.VMEM((tokens * KVH, HD), F32),
            pltpu.VMEM((KVH, tokens, HD), BF16),
            pltpu.VMEM((KVH, tokens, HD), BF16),
            pltpu.VMEM(queries.shape, BF16),
            pltpu.VMEM(new_keys.shape, BF16),
            pltpu.VMEM(new_values.shape, BF16),
            pltpu.SMEM(parents.shape, jnp.int32),
            pltpu.SMEM(lengths.shape, jnp.int32),
            pltpu.VMEM((rp, HD), F32),
            pltpu.VMEM((nc, nb, rp, HD), BF16),
            pltpu.VMEM((nb, 16, HD), BF16),
            pltpu.VMEM((units, nc, ur + 16, HD), BF16),
            pltpu.VMEM((units, nc, ur + 16, HD), BF16),
            pltpu.VMEM((units, nb, ur, HD), BF16),
            pltpu.VMEM((units, ur, HD), F32),
            pltpu.VMEM((nc, nb, quarter), F32),
            pltpu.VMEM((nc, nb, quarter), F32),
            dma((7,)),
            dma((units, nc)),
            dma((nb, nc)),
            dma((nc, nb)),
            dma((nb,)),
            dma((nb,)),
            dma((units, nc)),
            dma((units, nc)),
            dma((units, nb)),
            dma((units, nb)),
            dma((nc,)),
            dma((nc,)),
        ],
        compiler_params=pltpu.CompilerParams(
            collective_id=0, has_side_effects=True, vmem_limit_bytes=60 * 1024 * 1024
        ),
    )(queries, new_keys, new_values, cache_keys, cache_values, parents, lengths, out_weight)


def solution(mesh):
    placed = (
        P(("groups", "beam"), "ctx"),
        P(("groups", "beam"), None),
        P(("groups", "beam"), None),
        P(("groups", "beam"), "ctx", None, None),
        P(("groups", "beam"), "ctx", None, None),
        P("groups"),
        P("groups"),
        P("ctx", "beam"),
    )
    return jax.shard_map(
        functools.partial(per_device, mesh.shape["beam"], mesh.shape["ctx"]),
        mesh=mesh,
        in_specs=placed,
        out_specs=P("groups", ("beam", "ctx")),
        check_vma=False,
    )
```

```python
import functools
import math

import jax
import jax.numpy as jnp
from jax import lax
from jax.experimental import pallas as pl
from jax.experimental.pallas import tpu as pltpu
from jax.sharding import PartitionSpec as P

H = 128
KVH = 8
HD = 128
SPAN = 128
GROUP = H // KVH
LOWEST = -3.0e38
LANES = 128
MESH = pl.DeviceIdType.MESH
F32 = jnp.float32
BF16 = jnp.bfloat16


def split3(x):
    hi = x.astype(BF16).astype(F32)
    mid = (x - hi).astype(BF16).astype(F32)
    return hi, mid, x - hi - mid


def kernel(
    nb, nc, hs, rows_total, tokens,
    q_hbm, nk_hbm, nv_hbm, ck_hbm, cv_hbm, par_hbm, len_hbm, w_hbm,
    out_ref,
    w_vm, ck_vm, cv_vm, k32, v32, kh, vh,
    q_in, nk_in, nv_in, par_sm, len_sm,
    q_rows, q_buf, n_buf, d_send, d_recv, e_buf, a_rows, g_send, g_recv,
    in_sem, w_sem, qs_sem, qr_sem, ns_sem, nr_sem, ds_sem, dr_sem,
    es_sem, er_sem, gs_sem, gr_sem,
):
    g = lax.axis_index("groups")
    p = lax.axis_index("beam")
    c = lax.axis_index("ctx")
    rp = max(hs, GROUP)
    units = rp // GROUP
    ur = nb * GROUP
    quarter = w_vm.shape[2]

    def dev(b, s):
        return (g, b, s)

    def cmod(k):
        return lax.rem(c + k, nc)

    def pmod(j):
        return lax.rem(p + j, nb)

    loads = []
    for i, (src, dst) in enumerate(
        (
            (q_hbm, q_in), (nk_hbm, nk_in), (nv_hbm, nv_in),
            (par_hbm, par_sm), (len_hbm, len_sm),
            (ck_hbm.at[0], ck_vm), (cv_hbm.at[0], cv_vm),
        )
    ):
        load = pltpu.make_async_copy(src, dst, in_sem.at[i])
        load.start()
        loads.append(load)

    def w_load(k):
        s = cmod(k)
        return pltpu.make_async_copy(
            w_hbm.at[:, pl.ds(pl.multiple_of(s * quarter, quarter), quarter)],
            w_vm.at[s],
            w_sem.at[k],
        )

    order = [k for k in range(1, nc)] + [0]
    for k in order:
        w_load(k).start()

    barrier = pltpu.get_barrier_semaphore()

    def greet(i, carry):
        b = pmod(i // nc)
        s = cmod(lax.rem(i, nc))
        pl.semaphore_signal(barrier, inc=1, device_id=dev(b, s), device_id_type=MESH)
        return carry

    lax.fori_loop(1, nb * nc, greet, 0)

    for i in range(3):
        loads[i].wait()
    q_rows[...] = jnp.zeros_like(q_rows)
    q_flat = q_in[...].astype(F32)
    for h in range(hs):
        q_rows[h : h + 1, :] = q_flat[:, h * HD : (h + 1) * HD]
    q_buf[c, p] = q_rows[...].astype(BF16)
    kv0 = (c * hs) // GROUP
    row16 = lax.broadcasted_iota(jnp.int32, (16, HD), 0)
    staged = jnp.zeros((16, HD), F32)
    for u in range(units):
        lane0 = pl.multiple_of((kv0 + u) * HD, HD)
        staged = jnp.where(row16 == u, nk_in[:, pl.ds(lane0, HD)].astype(F32), staged)
        staged = jnp.where(row16 == 8 + u, nv_in[:, pl.ds(lane0, HD)].astype(F32), staged)
    n_buf[p] = staged.astype(BF16)

    pl.semaphore_wait(barrier, nb * nc - 1)

    def q_copy(j, k):
        return pltpu.make_async_remote_copy(
            src_ref=q_buf.at[c, p],
            dst_ref=q_buf.at[c, p],
            send_sem=qs_sem.at[j, k],
            recv_sem=qr_sem.at[c, p],
            device_id=dev(pmod(j), cmod(k)),
            device_id_type=MESH,
        )

    def n_copy(j):
        return pltpu.make_async_remote_copy(
            src_ref=n_buf.at[p],
            dst_ref=n_buf.at[p],
            send_sem=ns_sem.at[j],
            recv_sem=nr_sem.at[p],
            device_id=dev(pmod(j), c),
            device_id_type=MESH,
        )

    def q_arrival(b, s):
        return pltpu.make_async_remote_copy(
            src_ref=q_buf.at[s, b],
            dst_ref=q_buf.at[s, b],
            send_sem=qs_sem.at[0, 0],
            recv_sem=qr_sem.at[s, b],
            device_id=dev(pmod(1), c),
            device_id_type=MESH,
        )

    for k in range(nc - 1, -1, -1):
        for j in range(nb - 1, -1, -1):
            if j or k:
                q_copy(j, k).start()
    for j in range(nb - 1, 0, -1):
        n_copy(j).start()

    loads[5].wait()
    step = 64

    def widen(src, dst):
        def body(i, carry):
            t0 = pl.multiple_of(i * step, step)
            block = src[pl.ds(t0, step)].astype(F32)
            dst[pl.ds(pl.multiple_of(t0 * KVH, step * KVH), step * KVH), :] = block.reshape(
                step * KVH, HD
            )
            return carry

        lax.fori_loop(0, tokens // step, body, 0)

    widen(ck_vm, k32)
    for kv in range(KVH):
        kh[kv] = k32[pl.ds(kv, tokens, stride=KVH), :].astype(BF16)
    loads[6].wait()
    widen(cv_vm, v32)
    for kv in range(KVH):
        vh[kv] = v32[pl.ds(kv, tokens, stride=KVH), :].astype(BF16)
    loads[3].wait()
    loads[4].wait()
    limit = len_sm[p] * SPAN
    position = c * tokens + lax.broadcasted_iota(jnp.int32, (ur, tokens), 1)
    usable = position < limit
    scale = 1.0 / math.sqrt(HD)
    lane_u = lax.broadcasted_iota(jnp.int32, (ur, LANES), 1)
    row_u = lax.broadcasted_iota(jnp.int32, (ur, LANES), 0)
    row16 = lax.broadcasted_iota(jnp.int32, (16, LANES), 0)

    def to_lanes(column, u):
        return jnp.sum(jnp.where(lane_u == row_u + u * ur, column, 0.0), axis=0, keepdims=True)

    def attend(s):
        kv_base = (s * hs) // GROUP
        peak_row = jnp.zeros((1, LANES), F32)
        sum_row = jnp.zeros((1, LANES), F32)
        for u in range(units):
            q = jnp.concatenate(
                [q_buf[s, b, u * GROUP : (u + 1) * GROUP, :] for b in range(nb)], axis=0
            )
            scores = lax.dot_general(
                q, kh[kv_base + u], (((1,), (1,)), ((), ())), preferred_element_type=F32
            )
            scores = jnp.where(usable, scores * scale, -jnp.inf)
            peak = jnp.maximum(jnp.max(scores, axis=1, keepdims=True), LOWEST)
            weights = jnp.exp(scores - peak)
            total = jnp.sum(weights, axis=1, keepdims=True)
            blended = jnp.dot(weights.astype(BF16), vh[kv_base + u], preferred_element_type=F32)
            d_send[s, u * ur : (u + 1) * ur, :] = blended.astype(BF16)
            peak_row = peak_row + to_lanes(peak, u)
            sum_row = sum_row + to_lanes(total, u)
        stats = jnp.zeros((16, LANES), F32)
        for i, piece in enumerate(split3(peak_row) + split3(sum_row)):
            stats = jnp.where(row16 == i, piece, stats)
        d_send[s, units * ur : units * ur + 16, :] = stats.astype(BF16)

    def d_copy(k):
        return pltpu.make_async_remote_copy(
            src_ref=d_send.at[cmod(k)],
            dst_ref=d_recv.at[c],
            send_sem=ds_sem.at[k],
            recv_sem=dr_sem.at[c],
            device_id=dev(p, cmod(k)),
            device_id_type=MESH,
        )

    def d_arrival(s):
        return pltpu.make_async_remote_copy(
            src_ref=d_recv.at[s],
            dst_ref=d_recv.at[s],
            send_sem=ds_sem.at[0],
            recv_sem=dr_sem.at[s],
            device_id=dev(p, cmod(1)),
            device_id_type=MESH,
        )

    for k in order:
        s = cmod(k)
        for j in range(nb):
            if j or k:
                q_arrival(pmod(j), s).wait_recv()
        attend(s)
        if k:
            d_copy(k).start()

    for j in range(1, nb):
        pltpu.make_async_remote_copy(
            src_ref=n_buf.at[pmod(j)],
            dst_ref=n_buf.at[pmod(j)],
            send_sem=ns_sem.at[0],
            recv_sem=nr_sem.at[pmod(j)],
            device_id=dev(pmod(j), c),
            device_id_type=MESH,
        ).wait_recv()
    own_row = jnp.zeros((1, LANES), F32)
    own_values = []
    for u in range(units):
        own_scores = []
        for b in range(nb):
            fresh = n_buf[b].astype(F32)
            q = q_buf[c, b, u * GROUP : (u + 1) * GROUP, :].astype(F32)
            own_scores.append(jnp.sum(q * fresh[u : u + 1], axis=1, keepdims=True))
            own_values.append(jnp.broadcast_to(fresh[8 + u : 9 + u], (GROUP, HD)))
        own_row = own_row + to_lanes(
            jnp.broadcast_to(jnp.concatenate(own_scores, axis=0), (ur, LANES)), u
        )
    own_row = own_row * scale
    own_value = jnp.concatenate(own_values, axis=0)

    for k in range(1, nc):
        d_arrival(cmod(k)).wait_recv()
    rows = units * ur
    states = []
    for k in range(nc):
        ref = d_send if k == 0 else d_recv
        s = cmod(k)
        stats = ref[s, rows : rows + 16, :].astype(F32)
        states.append(
            (
                ref, s,
                stats[0:1] + stats[1:2] + stats[2:3],
                stats[3:4] + stats[4:5] + stats[5:6],
            )
        )
    top = own_row
    for _, _, peak, _ in states:
        top = jnp.maximum(top, peak)
    own_scale = jnp.exp(own_row - top)
    total = own_scale
    scales = []
    for _, _, peak, weight_sum in states:
        factor = jnp.exp(peak - top)
        scales.append(factor)
        total = total + weight_sum * factor
    inverse = 1.0 / total
    lane_r = lax.broadcasted_iota(jnp.int32, (rows, LANES), 1)
    row_r = lax.broadcasted_iota(jnp.int32, (rows, LANES), 0)
    diagonal = lane_r == row_r

    def to_rows(lanes):
        return jnp.sum(jnp.where(diagonal, lanes, 0.0), axis=1, keepdims=True)

    result = own_value * to_rows(own_scale * inverse)
    for (ref, s, _, _), factor in zip(states, scales):
        result = result + ref[s, 0:rows, :].astype(F32) * to_rows(factor * inverse)
    e_buf[p] = result.astype(BF16)

    def e_copy(j):
        return pltpu.make_async_remote_copy(
            src_ref=e_buf.at[p],
            dst_ref=e_buf.at[p],
            send_sem=es_sem.at[j],
            recv_sem=er_sem.at[p],
            device_id=dev(pmod(j), c),
            device_id_type=MESH,
        )

    for j in range(nb - 1, 0, -1):
        e_copy(j).start()
    for j in range(1, nb):
        pltpu.make_async_remote_copy(
            src_ref=e_buf.at[pmod(j)],
            dst_ref=e_buf.at[pmod(j)],
            send_sem=es_sem.at[0],
            recv_sem=er_sem.at[pmod(j)],
            device_id=dev(pmod(j), c),
            device_id_type=MESH,
        ).wait_recv()
    for b in range(nb):
        parent = par_sm[b]
        for u in range(units):
            r0 = u * ur + b * GROUP
            a_rows[r0 : r0 + GROUP, :] = e_buf[parent, r0 : r0 + GROUP, :].astype(F32)
    heads = []
    for h in range(hs):
        r0 = (h // GROUP) * ur + h % GROUP
        heads.append(a_rows[pl.ds(r0, nb, stride=GROUP), :])
    attended = jnp.concatenate(heads, axis=1).astype(BF16)

    def g_copy(k):
        return pltpu.make_async_remote_copy(
            src_ref=g_send.at[cmod(k)],
            dst_ref=g_recv.at[c],
            send_sem=gs_sem.at[k],
            recv_sem=gr_sem.at[c],
            device_id=dev(p, cmod(k)),
            device_id_type=MESH,
        )

    for k in order:
        s = cmod(k)
        w_load(k).wait()

        g_send[s] = jnp.dot(attended, w_vm[s], preferred_element_type=F32)
        if k:
            g_copy(k).start()
    total_out = g_send[c]
    for k in range(1, nc):
        s = cmod(k)
        pltpu.make_async_remote_copy(
            src_ref=g_recv.at[s],
            dst_ref=g_recv.at[s],
            send_sem=gs_sem.at[0],
            recv_sem=gr_sem.at[s],
            device_id=dev(p, cmod(1)),
            device_id_type=MESH,
        ).wait_recv()
        total_out = total_out + g_recv[s]
    out_ref[...] = total_out.astype(BF16)

    for k in range(nc):
        for j in range(nb):
            if j or k:
                q_copy(j, k).wait_send()
    for j in range(1, nb):
        n_copy(j).wait_send()
        e_copy(j).wait_send()
    for k in range(1, nc):
        d_copy(k).wait_send()
        g_copy(k).wait_send()


def per_device(nb, nc, queries, new_keys, new_values, cache_keys, cache_values, parents, lengths, out_weight):
    hs = queries.shape[1] // HD
    tokens = cache_keys.shape[1]
    rp = max(hs, GROUP)
    rows = (rp // GROUP) * nb * GROUP
    depth, columns = out_weight.shape
    quarter = columns // nc
    dma = pltpu.SemaphoreType.DMA
    return pl.pallas_call(
        functools.partial(kernel, nb, nc, hs, rows, tokens),
        out_shape=pltpu.VMEM((nb, quarter), BF16),
        in_specs=[pl.BlockSpec(memory_space=pltpu.HBM)] * 8,
        out_specs=pl.BlockSpec(memory_space=pltpu.VMEM),
        scratch_shapes=[
            pltpu.VMEM((nc, depth, quarter), BF16),
            pltpu.VMEM((tokens, KVH, HD), BF16),
            pltpu.VMEM((tokens, KVH, HD), BF16),
            pltpu.VMEM((tokens * KVH, HD), F32),
            pltpu.VMEM((tokens * KVH, HD), F32),
            pltpu.VMEM((KVH, tokens, HD), BF16),
            pltpu.VMEM((KVH, tokens, HD), BF16),
            pltpu.VMEM(queries.shape, BF16),
            pltpu.VMEM(new_keys.shape, BF16),
            pltpu.VMEM(new_values.shape, BF16),
            pltpu.SMEM(parents.shape, jnp.int32),
            pltpu.SMEM(lengths.shape, jnp.int32),
            pltpu.VMEM((rp, HD), F32),
            pltpu.VMEM((nc, nb, rp, HD), BF16),
            pltpu.VMEM((nb, 16, HD), BF16),
            pltpu.VMEM((nc, rows + 16, HD), BF16),
            pltpu.VMEM((nc, rows + 16, HD), BF16),
            pltpu.VMEM((nb, rows, HD), BF16),
            pltpu.VMEM((rows, HD), F32),
            pltpu.VMEM((nc, nb, quarter), F32),
            pltpu.VMEM((nc, nb, quarter), F32),
            dma((7,)),
            dma((nc,)),
            dma((nb, nc)),
            dma((nc, nb)),
            dma((nb,)),
            dma((nb,)),
            dma((nc,)),
            dma((nc,)),
            dma((nb,)),
            dma((nb,)),
            dma((nc,)),
            dma((nc,)),
        ],
        compiler_params=pltpu.CompilerParams(
            collective_id=0, has_side_effects=True, vmem_limit_bytes=60 * 1024 * 1024
        ),
    )(queries, new_keys, new_values, cache_keys, cache_values, parents, lengths, out_weight)


def solution(mesh):
    placed = (
        P(("groups", "beam"), "ctx"),
        P(("groups", "beam"), None),
        P(("groups", "beam"), None),
        P(("groups", "beam"), "ctx", None, None),
        P(("groups", "beam"), "ctx", None, None),
        P("groups"),
        P("groups"),
        P("ctx", "beam"),
    )
    return jax.shard_map(
        functools.partial(per_device, mesh.shape["beam"], mesh.shape["ctx"]),
        mesh=mesh,
        in_specs=placed,
        out_specs=P("groups", ("beam", "ctx")),
        check_vma=False,
    )
```

```python
import functools
import math

import jax
import jax.numpy as jnp
from jax import lax
from jax.experimental import pallas as pl
from jax.experimental.pallas import tpu as pltpu
from jax.sharding import PartitionSpec as P

H = 128
KVH = 8
HD = 128
SPAN = 128
GROUP = H // KVH
LOWEST = -3.0e38
LANES = 128
MESH = pl.DeviceIdType.MESH
F32 = jnp.float32
BF16 = jnp.bfloat16


def split3(x):
    hi = x.astype(BF16).astype(F32)
    mid = (x - hi).astype(BF16).astype(F32)
    return hi, mid, x - hi - mid


def kernel(
    nb, nc, hs, rows_total, tokens,
    q_hbm, nk_hbm, nv_hbm, ck_hbm, cv_hbm, par_hbm, len_hbm, w_hbm,
    out_ref,
    w_vm, ck_vm, cv_vm, k32, v32, kh, vh,
    q_in, nk_in, nv_in, par_sm, len_sm,
    q_rows, q_buf, n_buf, d_send, d_recv, e_buf, a_rows, g_send, g_recv,
    in_sem, w_sem, qs_sem, qr_sem, ns_sem, nr_sem, ds_sem, dr_sem,
    es_sem, er_sem, gs_sem, gr_sem,
):
    g = lax.axis_index("groups")
    p = lax.axis_index("beam")
    c = lax.axis_index("ctx")
    rp = max(hs, GROUP)
    units = rp // GROUP
    ur = nb * GROUP
    quarter = w_vm.shape[2]

    def dev(b, s):
        return (g, b, s)

    def cmod(k):
        return lax.rem(c + k, nc)

    def pmod(j):
        return lax.rem(p + j, nb)

    loads = []
    for i, (src, dst) in enumerate(
        (
            (q_hbm, q_in), (nk_hbm, nk_in), (nv_hbm, nv_in),
            (par_hbm, par_sm), (len_hbm, len_sm),
            (ck_hbm.at[0], ck_vm), (cv_hbm.at[0], cv_vm),
        )
    ):
        load = pltpu.make_async_copy(src, dst, in_sem.at[i])
        load.start()
        loads.append(load)

    def w_load(k):
        s = cmod(k)
        return pltpu.make_async_copy(
            w_hbm.at[:, pl.ds(pl.multiple_of(s * quarter, quarter), quarter)],
            w_vm.at[s],
            w_sem.at[k],
        )

    order = [k for k in range(1, nc)] + [0]
    for k in order:
        w_load(k).start()

    barrier = pltpu.get_barrier_semaphore()

    def greet(i, carry):
        b = pmod(i // nc)
        s = cmod(lax.rem(i, nc))
        pl.semaphore_signal(barrier, inc=1, device_id=dev(b, s), device_id_type=MESH)
        return carry

    lax.fori_loop(1, nb * nc, greet, 0)

    for i in range(3):
        loads[i].wait()
    q_rows[...] = jnp.zeros_like(q_rows)
    q_flat = q_in[...].astype(F32)
    for h in range(hs):
        q_rows[h : h + 1, :] = q_flat[:, h * HD : (h + 1) * HD]
    q_buf[c, p] = q_rows[...].astype(BF16)
    kv0 = (c * hs) // GROUP
    row16 = lax.broadcasted_iota(jnp.int32, (16, HD), 0)
    staged = jnp.zeros((16, HD), F32)
    for u in range(units):
        lane0 = pl.multiple_of((kv0 + u) * HD, HD)
        staged = jnp.where(row16 == u, nk_in[:, pl.ds(lane0, HD)].astype(F32), staged)
        staged = jnp.where(row16 == 8 + u, nv_in[:, pl.ds(lane0, HD)].astype(F32), staged)
    n_buf[p] = staged.astype(BF16)

    pl.semaphore_wait(barrier, nb * nc - 1)

    def q_copy(j, k):
        return pltpu.make_async_remote_copy(
            src_ref=q_buf.at[c, p],
            dst_ref=q_buf.at[c, p],
            send_sem=qs_sem.at[j, k],
            recv_sem=qr_sem.at[c, p],
            device_id=dev(pmod(j), cmod(k)),
            device_id_type=MESH,
        )

    def n_copy(j):
        return pltpu.make_async_remote_copy(
            src_ref=n_buf.at[p],
            dst_ref=n_buf.at[p],
            send_sem=ns_sem.at[j],
            recv_sem=nr_sem.at[p],
            device_id=dev(pmod(j), c),
            device_id_type=MESH,
        )

    def q_arrival(b, s):
        return pltpu.make_async_remote_copy(
            src_ref=q_buf.at[s, b],
            dst_ref=q_buf.at[s, b],
            send_sem=qs_sem.at[0, 0],
            recv_sem=qr_sem.at[s, b],
            device_id=dev(pmod(1), c),
            device_id_type=MESH,
        )

    for k in range(nc - 1, -1, -1):
        for j in range(nb - 1, -1, -1):
            if j or k:
                q_copy(j, k).start()
    for j in range(nb - 1, 0, -1):
        n_copy(j).start()

    loads[5].wait()
    step = 64

    def widen(src, dst):
        def body(i, carry):
            t0 = pl.multiple_of(i * step, step)
            block = src[pl.ds(t0, step)].astype(F32)
            dst[pl.ds(pl.multiple_of(t0 * KVH, step * KVH), step * KVH), :] = block.reshape(
                step * KVH, HD
            )
            return carry

        lax.fori_loop(0, tokens // step, body, 0)

    widen(ck_vm, k32)
    for kv in range(KVH):
        u0 = (kv % units) * HD
        kh[kv // units, :, u0 : u0 + HD] = k32[pl.ds(kv, tokens, stride=KVH), :].astype(BF16)
    loads[6].wait()
    widen(cv_vm, v32)
    for kv in range(KVH):
        u0 = (kv % units) * HD
        vh[kv // units, u0 : u0 + HD, :] = jnp.transpose(
            v32[pl.ds(kv, tokens, stride=KVH), :].astype(BF16)
        )
    loads[3].wait()
    loads[4].wait()
    limit = len_sm[p] * SPAN
    position = c * tokens + lax.broadcasted_iota(jnp.int32, (tokens, LANES), 0)
    usable = position < limit
    scale = 1.0 / math.sqrt(HD)
    lane_u = lax.broadcasted_iota(jnp.int32, (ur, LANES), 1)
    row_u = lax.broadcasted_iota(jnp.int32, (ur, LANES), 0)
    row16 = lax.broadcasted_iota(jnp.int32, (16, LANES), 0)

    def to_lanes(column, u):
        return jnp.sum(jnp.where(lane_u == row_u + u * ur, column, 0.0), axis=0, keepdims=True)

    lane_d = lax.broadcasted_iota(jnp.int32, (HD, LANES), 1)

    def attend(s):
        pair = (s * hs) // GROUP // units
        bands = []
        for u in range(units):
            q = jnp.concatenate(
                [q_buf[s, b, u * GROUP : (u + 1) * GROUP, :] for b in range(nb)], axis=0
            )
            bands.append(
                jnp.concatenate([q if v == u else jnp.zeros_like(q) for v in range(units)], axis=1)
            )
        scores = lax.dot_general(
            kh[pair], jnp.concatenate(bands, axis=0), (((1,), (1,)), ((), ())),
            preferred_element_type=F32,
        )
        scores = jnp.where(usable, scores * scale, -jnp.inf)
        peak = jnp.maximum(jnp.max(scores, axis=0, keepdims=True), LOWEST)
        weights = jnp.exp(scores - peak)
        total = jnp.sum(weights, axis=0, keepdims=True)
        both = jnp.dot(vh[pair], weights.astype(BF16), preferred_element_type=F32)
        blended = both[0:HD]
        for u in range(1, units):
            blended = jnp.where(lane_d >= u * ur, both[u * HD : (u + 1) * HD], blended)
        d_send[s, 0:HD, :] = blended.astype(BF16)
        stats = jnp.zeros((16, LANES), F32)
        for i, piece in enumerate(split3(peak) + split3(total)):
            stats = jnp.where(row16 == i, piece, stats)
        d_send[s, HD : HD + 16, :] = stats.astype(BF16)

    def d_copy(k):
        return pltpu.make_async_remote_copy(
            src_ref=d_send.at[cmod(k)],
            dst_ref=d_recv.at[c],
            send_sem=ds_sem.at[k],
            recv_sem=dr_sem.at[c],
            device_id=dev(p, cmod(k)),
            device_id_type=MESH,
        )

    def d_arrival(s):
        return pltpu.make_async_remote_copy(
            src_ref=d_recv.at[s],
            dst_ref=d_recv.at[s],
            send_sem=ds_sem.at[0],
            recv_sem=dr_sem.at[s],
            device_id=dev(p, cmod(1)),
            device_id_type=MESH,
        )

    for k in order:
        s = cmod(k)
        for j in range(nb):
            if j or k:
                q_arrival(pmod(j), s).wait_recv()
        attend(s)
        if k:
            d_copy(k).start()

    for j in range(1, nb):
        pltpu.make_async_remote_copy(
            src_ref=n_buf.at[pmod(j)],
            dst_ref=n_buf.at[pmod(j)],
            send_sem=ns_sem.at[0],
            recv_sem=nr_sem.at[pmod(j)],
            device_id=dev(pmod(j), c),
            device_id_type=MESH,
        ).wait_recv()
    own_row = jnp.zeros((1, LANES), F32)
    own_values = []
    for u in range(units):
        own_scores = []
        for b in range(nb):
            fresh = n_buf[b].astype(F32)
            q = q_buf[c, b, u * GROUP : (u + 1) * GROUP, :].astype(F32)
            own_scores.append(jnp.sum(q * fresh[u : u + 1], axis=1, keepdims=True))
            own_values.append(jnp.broadcast_to(fresh[8 + u : 9 + u], (GROUP, HD)))
        own_row = own_row + to_lanes(
            jnp.broadcast_to(jnp.concatenate(own_scores, axis=0), (ur, LANES)), u
        )
    own_row = own_row * scale
    own_value = jnp.transpose(jnp.concatenate(own_values, axis=0))

    for k in range(1, nc):
        d_arrival(cmod(k)).wait_recv()
    states = []
    for k in range(nc):
        ref = d_send if k == 0 else d_recv
        s = cmod(k)
        stats = ref[s, HD : HD + 16, :].astype(F32)
        states.append(
            (
                ref, s,
                stats[0:1] + stats[1:2] + stats[2:3],
                stats[3:4] + stats[4:5] + stats[5:6],
            )
        )
    top = own_row
    for _, _, peak, _ in states:
        top = jnp.maximum(top, peak)
    own_scale = jnp.exp(own_row - top)
    total = own_scale
    scales = []
    for _, _, peak, weight_sum in states:
        factor = jnp.exp(peak - top)
        scales.append(factor)
        total = total + weight_sum * factor
    inverse = 1.0 / total
    result = own_value * (own_scale * inverse)
    for (ref, s, _, _), factor in zip(states, scales):
        result = result + ref[s, 0:HD, :].astype(F32) * (factor * inverse)
    e_buf[p] = jnp.transpose(result).astype(BF16)

    def e_copy(j):
        return pltpu.make_async_remote_copy(
            src_ref=e_buf.at[p],
            dst_ref=e_buf.at[p],
            send_sem=es_sem.at[j],
            recv_sem=er_sem.at[p],
            device_id=dev(pmod(j), c),
            device_id_type=MESH,
        )

    for j in range(nb - 1, 0, -1):
        e_copy(j).start()
    for j in range(1, nb):
        pltpu.make_async_remote_copy(
            src_ref=e_buf.at[pmod(j)],
            dst_ref=e_buf.at[pmod(j)],
            send_sem=es_sem.at[0],
            recv_sem=er_sem.at[pmod(j)],
            device_id=dev(pmod(j), c),
            device_id_type=MESH,
        ).wait_recv()
    for b in range(nb):
        parent = par_sm[b]
        for u in range(units):
            r0 = u * ur + b * GROUP
            a_rows[r0 : r0 + GROUP, :] = e_buf[parent, r0 : r0 + GROUP, :].astype(F32)
    heads = []
    for h in range(hs):
        r0 = (h // GROUP) * ur + h % GROUP
        heads.append(a_rows[pl.ds(r0, nb, stride=GROUP), :])
    attended = jnp.concatenate(heads, axis=1).astype(BF16)

    def g_copy(k):
        return pltpu.make_async_remote_copy(
            src_ref=g_send.at[cmod(k)],
            dst_ref=g_recv.at[c],
            send_sem=gs_sem.at[k],
            recv_sem=gr_sem.at[c],
            device_id=dev(p, cmod(k)),
            device_id_type=MESH,
        )

    for k in order:
        s = cmod(k)
        w_load(k).wait()

        g_send[s] = jnp.dot(attended, w_vm[s], preferred_element_type=F32)
        if k:
            g_copy(k).start()
    total_out = g_send[c]
    for k in range(1, nc):
        s = cmod(k)
        pltpu.make_async_remote_copy(
            src_ref=g_recv.at[s],
            dst_ref=g_recv.at[s],
            send_sem=gs_sem.at[0],
            recv_sem=gr_sem.at[s],
            device_id=dev(p, cmod(1)),
            device_id_type=MESH,
        ).wait_recv()
        total_out = total_out + g_recv[s]
    out_ref[...] = total_out.astype(BF16)

    for k in range(nc):
        for j in range(nb):
            if j or k:
                q_copy(j, k).wait_send()
    for j in range(1, nb):
        n_copy(j).wait_send()
        e_copy(j).wait_send()
    for k in range(1, nc):
        d_copy(k).wait_send()
        g_copy(k).wait_send()


def per_device(nb, nc, queries, new_keys, new_values, cache_keys, cache_values, parents, lengths, out_weight):
    hs = queries.shape[1] // HD
    tokens = cache_keys.shape[1]
    rp = max(hs, GROUP)
    units = rp // GROUP
    rows = units * nb * GROUP
    depth, columns = out_weight.shape
    quarter = columns // nc
    dma = pltpu.SemaphoreType.DMA
    return pl.pallas_call(
        functools.partial(kernel, nb, nc, hs, rows, tokens),
        out_shape=pltpu.VMEM((nb, quarter), BF16),
        in_specs=[pl.BlockSpec(memory_space=pltpu.HBM)] * 8,
        out_specs=pl.BlockSpec(memory_space=pltpu.VMEM),
        scratch_shapes=[
            pltpu.VMEM((nc, depth, quarter), BF16),
            pltpu.VMEM((tokens, KVH, HD), BF16),
            pltpu.VMEM((tokens, KVH, HD), BF16),
            pltpu.VMEM((tokens * KVH, HD), F32),
            pltpu.VMEM((tokens * KVH, HD), F32),
            pltpu.VMEM((KVH // units, tokens, units * HD), BF16),
            pltpu.VMEM((KVH // units, units * HD, tokens), BF16),
            pltpu.VMEM(queries.shape, BF16),
            pltpu.VMEM(new_keys.shape, BF16),
            pltpu.VMEM(new_values.shape, BF16),
            pltpu.SMEM(parents.shape, jnp.int32),
            pltpu.SMEM(lengths.shape, jnp.int32),
            pltpu.VMEM((rp, HD), F32),
            pltpu.VMEM((nc, nb, rp, HD), BF16),
            pltpu.VMEM((nb, 16, HD), BF16),
            pltpu.VMEM((nc, HD + 16, rows), BF16),
            pltpu.VMEM((nc, HD + 16, rows), BF16),
            pltpu.VMEM((nb, rows, HD), BF16),
            pltpu.VMEM((rows, HD), F32),
            pltpu.VMEM((nc, nb, quarter), F32),
            pltpu.VMEM((nc, nb, quarter), F32),
            dma((7,)),
            dma((nc,)),
            dma((nb, nc)),
            dma((nc, nb)),
            dma((nb,)),
            dma((nb,)),
            dma((nc,)),
            dma((nc,)),
            dma((nb,)),
            dma((nb,)),
            dma((nc,)),
            dma((nc,)),
        ],
        compiler_params=pltpu.CompilerParams(
            collective_id=0, has_side_effects=True, vmem_limit_bytes=60 * 1024 * 1024
        ),
    )(queries, new_keys, new_values, cache_keys, cache_values, parents, lengths, out_weight)


def solution(mesh):
    placed = (
        P(("groups", "beam"), "ctx"),
        P(("groups", "beam"), None),
        P(("groups", "beam"), None),
        P(("groups", "beam"), "ctx", None, None),
        P(("groups", "beam"), "ctx", None, None),
        P("groups"),
        P("groups"),
        P("ctx", "beam"),
    )
    return jax.shard_map(
        functools.partial(per_device, mesh.shape["beam"], mesh.shape["ctx"]),
        mesh=mesh,
        in_specs=placed,
        out_specs=P("groups", ("beam", "ctx")),
        check_vma=False,
    )
```

```python
import functools
import math

import jax
import jax.numpy as jnp
from jax import lax
from jax.experimental import pallas as pl
from jax.experimental.pallas import tpu as pltpu
from jax.sharding import PartitionSpec as P

H = 128
KVH = 8
HD = 128
SPAN = 128
GROUP = H // KVH
LOWEST = -3.0e38
LANES = 128
MESH = pl.DeviceIdType.MESH
F32 = jnp.float32
BF16 = jnp.bfloat16


def split3(x):
    hi = x.astype(BF16).astype(F32)
    mid = (x - hi).astype(BF16).astype(F32)
    return hi, mid, x - hi - mid


def kernel(
    nb, nc, hs, rows_total, tokens,
    q_hbm, nk_hbm, nv_hbm, ck_hbm, cv_hbm, par_hbm, len_hbm, w_hbm,
    out_ref,
    w_vm, ck_vm, cv_vm, k32, v32, kh, vh,
    q_in, nk_in, nv_in, par_sm, len_sm,
    q_rows, q_buf, n_buf, d_send, d_recv, e_buf, a_rows, g_send, g_recv,
    in_sem, w_sem, qs_sem, qr_sem, ns_sem, nr_sem, ds_sem, dr_sem,
    es_sem, er_sem, gs_sem, gr_sem,
):
    g = lax.axis_index("groups")
    p = lax.axis_index("beam")
    c = lax.axis_index("ctx")
    rp = max(hs, GROUP)
    units = rp // GROUP
    ur = nb * GROUP
    quarter = w_vm.shape[2]

    def dev(b, s):
        return (g, b, s)

    def cmod(k):
        return 2 * lax.rem(c // 2 + k // 2, nc // 2) + lax.rem(c + k, 2)

    def pmod(j):
        return lax.rem(p + j, nb)

    loads = []
    for i, (src, dst) in enumerate(
        (
            (q_hbm, q_in), (nk_hbm, nk_in), (nv_hbm, nv_in),
            (par_hbm, par_sm), (len_hbm, len_sm),
            (ck_hbm.at[0], ck_vm), (cv_hbm.at[0], cv_vm),
        )
    ):
        loads.append(pltpu.make_async_copy(src, dst, in_sem.at[i]))
    for load in loads[:3]:
        load.start()

    def w_load(k):
        s = cmod(k)
        return pltpu.make_async_copy(
            w_hbm.at[:, pl.ds(pl.multiple_of(s * quarter, quarter), quarter)],
            w_vm.at[s],
            w_sem.at[k],
        )

    order = [k for k in range(nc - 1, -1, -1)]

    barrier = pltpu.get_barrier_semaphore()

    def greet(i, carry):
        b = pmod(i // nc)
        s = cmod(lax.rem(i, nc))
        pl.semaphore_signal(barrier, inc=1, device_id=dev(b, s), device_id_type=MESH)
        return carry

    lax.fori_loop(1, nb * nc, greet, 0)

    for load in loads[5:] + loads[3:5]:
        load.start()
    for k in order:
        w_load(k).start()

    for i in range(3):
        loads[i].wait()
    q_rows[...] = jnp.zeros_like(q_rows)
    q_flat = q_in[...].astype(F32)
    for h in range(hs):
        q_rows[h : h + 1, :] = q_flat[:, h * HD : (h + 1) * HD]
    q_buf[c, p] = q_rows[...].astype(BF16)
    kv0 = (c * hs) // GROUP
    row16 = lax.broadcasted_iota(jnp.int32, (16, HD), 0)
    staged = jnp.zeros((16, HD), F32)
    for u in range(units):
        lane0 = pl.multiple_of((kv0 + u) * HD, HD)
        staged = jnp.where(row16 == u, nk_in[:, pl.ds(lane0, HD)].astype(F32), staged)
        staged = jnp.where(row16 == 8 + u, nv_in[:, pl.ds(lane0, HD)].astype(F32), staged)
    n_buf[p] = staged.astype(BF16)

    pl.semaphore_wait(barrier, nb * nc - 1)

    def q_copy(j, k):
        return pltpu.make_async_remote_copy(
            src_ref=q_buf.at[c, p],
            dst_ref=q_buf.at[c, p],
            send_sem=qs_sem.at[j, k],
            recv_sem=qr_sem.at[c, p],
            device_id=dev(pmod(j), cmod(k)),
            device_id_type=MESH,
        )

    def n_copy(j):
        return pltpu.make_async_remote_copy(
            src_ref=n_buf.at[p],
            dst_ref=n_buf.at[p],
            send_sem=ns_sem.at[j],
            recv_sem=nr_sem.at[p],
            device_id=dev(pmod(j), c),
            device_id_type=MESH,
        )

    def q_arrival(b, s):
        return pltpu.make_async_remote_copy(
            src_ref=q_buf.at[s, b],
            dst_ref=q_buf.at[s, b],
            send_sem=qs_sem.at[0, 0],
            recv_sem=qr_sem.at[s, b],
            device_id=dev(pmod(1), c),
            device_id_type=MESH,
        )

    for k in range(nc - 1, -1, -1):
        for j in range(nb - 1, -1, -1):
            if j or k:
                q_copy(j, k).start()
    for j in range(nb - 1, 0, -1):
        n_copy(j).start()

    loads[5].wait()
    step = 64

    def widen(src, dst):
        def body(i, carry):
            t0 = pl.multiple_of(i * step, step)
            block = src[pl.ds(t0, step)].astype(F32)
            dst[pl.ds(pl.multiple_of(t0 * KVH, step * KVH), step * KVH), :] = block.reshape(
                step * KVH, HD
            )
            return carry

        lax.fori_loop(0, tokens // step, body, 0)

    widen(ck_vm, k32)
    for kv in range(KVH):
        u0 = (kv % units) * HD
        kh[kv // units, :, u0 : u0 + HD] = k32[pl.ds(kv, tokens, stride=KVH), :].astype(BF16)
    loads[6].wait()
    widen(cv_vm, v32)
    for kv in range(KVH):
        u0 = (kv % units) * HD
        vh[kv // units, u0 : u0 + HD, :] = jnp.transpose(
            v32[pl.ds(kv, tokens, stride=KVH), :].astype(BF16)
        )
    loads[3].wait()
    loads[4].wait()
    limit = len_sm[p] * SPAN
    position = c * tokens + lax.broadcasted_iota(jnp.int32, (tokens, LANES), 0)
    usable = position < limit
    scale = 1.0 / math.sqrt(HD)
    lane_u = lax.broadcasted_iota(jnp.int32, (ur, LANES), 1)
    row_u = lax.broadcasted_iota(jnp.int32, (ur, LANES), 0)
    row16 = lax.broadcasted_iota(jnp.int32, (16, LANES), 0)

    def to_lanes(column, u):
        return jnp.sum(jnp.where(lane_u == row_u + u * ur, column, 0.0), axis=0, keepdims=True)

    lane_d = lax.broadcasted_iota(jnp.int32, (HD, LANES), 1)

    def attend(s):
        pair = (s * hs) // GROUP // units
        bands = []
        for u in range(units):
            q = jnp.concatenate(
                [q_buf[s, b, u * GROUP : (u + 1) * GROUP, :] for b in range(nb)], axis=0
            )
            bands.append(
                jnp.concatenate([q if v == u else jnp.zeros_like(q) for v in range(units)], axis=1)
            )
        scores = lax.dot_general(
            kh[pair], jnp.concatenate(bands, axis=0), (((1,), (1,)), ((), ())),
            preferred_element_type=F32,
        )
        scores = jnp.where(usable, scores * scale, -jnp.inf)
        peak = jnp.maximum(jnp.max(scores, axis=0, keepdims=True), LOWEST)
        weights = jnp.exp(scores - peak)
        total = jnp.sum(weights, axis=0, keepdims=True)
        both = jnp.dot(vh[pair], weights.astype(BF16), preferred_element_type=F32)
        blended = both[0:HD]
        for u in range(1, units):
            blended = jnp.where(lane_d >= u * ur, both[u * HD : (u + 1) * HD], blended)
        d_send[s, 0:HD, :] = blended.astype(BF16)
        stats = jnp.zeros((16, LANES), F32)
        for i, piece in enumerate(split3(peak) + split3(total)):
            stats = jnp.where(row16 == i, piece, stats)
        d_send[s, HD : HD + 16, :] = stats.astype(BF16)

    def d_copy(k):
        return pltpu.make_async_remote_copy(
            src_ref=d_send.at[cmod(k)],
            dst_ref=d_recv.at[c],
            send_sem=ds_sem.at[k],
            recv_sem=dr_sem.at[c],
            device_id=dev(p, cmod(k)),
            device_id_type=MESH,
        )

    def d_arrival(s):
        return pltpu.make_async_remote_copy(
            src_ref=d_recv.at[s],
            dst_ref=d_recv.at[s],
            send_sem=ds_sem.at[0],
            recv_sem=dr_sem.at[s],
            device_id=dev(p, cmod(1)),
            device_id_type=MESH,
        )

    for k in order:
        s = cmod(k)
        for j in range(nb):
            if j or k:
                q_arrival(pmod(j), s).wait_recv()
        attend(s)
        if k:
            d_copy(k).start()

    for j in range(1, nb):
        pltpu.make_async_remote_copy(
            src_ref=n_buf.at[pmod(j)],
            dst_ref=n_buf.at[pmod(j)],
            send_sem=ns_sem.at[0],
            recv_sem=nr_sem.at[pmod(j)],
            device_id=dev(pmod(j), c),
            device_id_type=MESH,
        ).wait_recv()
    own_row = jnp.zeros((1, LANES), F32)
    own_values = []
    for u in range(units):
        own_scores = []
        for b in range(nb):
            fresh = n_buf[b].astype(F32)
            q = q_buf[c, b, u * GROUP : (u + 1) * GROUP, :].astype(F32)
            own_scores.append(jnp.sum(q * fresh[u : u + 1], axis=1, keepdims=True))
            own_values.append(jnp.broadcast_to(fresh[8 + u : 9 + u], (GROUP, HD)))
        own_row = own_row + to_lanes(
            jnp.broadcast_to(jnp.concatenate(own_scores, axis=0), (ur, LANES)), u
        )
    own_row = own_row * scale
    own_value = jnp.transpose(jnp.concatenate(own_values, axis=0))

    for k in range(1, nc):
        d_arrival(cmod(k)).wait_recv()
    states = []
    for k in range(nc):
        ref = d_send if k == 0 else d_recv
        s = cmod(k)
        stats = ref[s, HD : HD + 16, :].astype(F32)
        states.append(
            (
                ref, s,
                stats[0:1] + stats[1:2] + stats[2:3],
                stats[3:4] + stats[4:5] + stats[5:6],
            )
        )
    top = own_row
    for _, _, peak, _ in states:
        top = jnp.maximum(top, peak)
    own_scale = jnp.exp(own_row - top)
    total = own_scale
    scales = []
    for _, _, peak, weight_sum in states:
        factor = jnp.exp(peak - top)
        scales.append(factor)
        total = total + weight_sum * factor
    inverse = 1.0 / total
    result = own_value * (own_scale * inverse)
    for (ref, s, _, _), factor in zip(states, scales):
        result = result + ref[s, 0:HD, :].astype(F32) * (factor * inverse)
    e_buf[p] = jnp.transpose(result).astype(BF16)

    def e_copy(j):
        return pltpu.make_async_remote_copy(
            src_ref=e_buf.at[p],
            dst_ref=e_buf.at[p],
            send_sem=es_sem.at[j],
            recv_sem=er_sem.at[p],
            device_id=dev(pmod(j), c),
            device_id_type=MESH,
        )

    for j in range(nb - 1, 0, -1):
        e_copy(j).start()
    for j in range(1, nb):
        pltpu.make_async_remote_copy(
            src_ref=e_buf.at[pmod(j)],
            dst_ref=e_buf.at[pmod(j)],
            send_sem=es_sem.at[0],
            recv_sem=er_sem.at[pmod(j)],
            device_id=dev(pmod(j), c),
            device_id_type=MESH,
        ).wait_recv()
    for b in range(nb):
        parent = par_sm[b]
        for u in range(units):
            r0 = u * ur + b * GROUP
            a_rows[r0 : r0 + GROUP, :] = e_buf[parent, r0 : r0 + GROUP, :].astype(F32)
    heads = []
    for h in range(hs):
        r0 = (h // GROUP) * ur + h % GROUP
        heads.append(a_rows[pl.ds(r0, nb, stride=GROUP), :])
    attended = jnp.concatenate(heads, axis=1).astype(BF16)

    def g_copy(k):
        return pltpu.make_async_remote_copy(
            src_ref=g_send.at[cmod(k)],
            dst_ref=g_recv.at[c],
            send_sem=gs_sem.at[k],
            recv_sem=gr_sem.at[c],
            device_id=dev(p, cmod(k)),
            device_id_type=MESH,
        )

    for k in order:
        s = cmod(k)
        w_load(k).wait()

        g_send[s] = jnp.dot(attended, w_vm[s], preferred_element_type=F32)
        if k:
            g_copy(k).start()
    total_out = g_send[c]
    for k in range(1, nc):
        s = cmod(k)
        pltpu.make_async_remote_copy(
            src_ref=g_recv.at[s],
            dst_ref=g_recv.at[s],
            send_sem=gs_sem.at[0],
            recv_sem=gr_sem.at[s],
            device_id=dev(p, cmod(1)),
            device_id_type=MESH,
        ).wait_recv()
        total_out = total_out + g_recv[s]
    out_ref[...] = total_out.astype(BF16)

    for k in range(nc):
        for j in range(nb):
            if j or k:
                q_copy(j, k).wait_send()
    for j in range(1, nb):
        n_copy(j).wait_send()
        e_copy(j).wait_send()
    for k in range(1, nc):
        d_copy(k).wait_send()
        g_copy(k).wait_send()


def per_device(nb, nc, queries, new_keys, new_values, cache_keys, cache_values, parents, lengths, out_weight):
    hs = queries.shape[1] // HD
    tokens = cache_keys.shape[1]
    rp = max(hs, GROUP)
    units = rp // GROUP
    rows = units * nb * GROUP
    depth, columns = out_weight.shape
    quarter = columns // nc
    dma = pltpu.SemaphoreType.DMA
    return pl.pallas_call(
        functools.partial(kernel, nb, nc, hs, rows, tokens),
        out_shape=pltpu.VMEM((nb, quarter), BF16),
        in_specs=[pl.BlockSpec(memory_space=pltpu.HBM)] * 8,
        out_specs=pl.BlockSpec(memory_space=pltpu.VMEM),
        scratch_shapes=[
            pltpu.VMEM((nc, depth, quarter), BF16),
            pltpu.VMEM((tokens, KVH, HD), BF16),
            pltpu.VMEM((tokens, KVH, HD), BF16),
            pltpu.VMEM((tokens * KVH, HD), F32),
            pltpu.VMEM((tokens * KVH, HD), F32),
            pltpu.VMEM((KVH // units, tokens, units * HD), BF16),
            pltpu.VMEM((KVH // units, units * HD, tokens), BF16),
            pltpu.VMEM(queries.shape, BF16),
            pltpu.VMEM(new_keys.shape, BF16),
            pltpu.VMEM(new_values.shape, BF16),
            pltpu.SMEM(parents.shape, jnp.int32),
            pltpu.SMEM(lengths.shape, jnp.int32),
            pltpu.VMEM((rp, HD), F32),
            pltpu.VMEM((nc, nb, rp, HD), BF16),
            pltpu.VMEM((nb, 16, HD), BF16),
            pltpu.VMEM((nc, HD + 16, rows), BF16),
            pltpu.VMEM((nc, HD + 16, rows), BF16),
            pltpu.VMEM((nb, rows, HD), BF16),
            pltpu.VMEM((rows, HD), F32),
            pltpu.VMEM((nc, nb, quarter), F32),
            pltpu.VMEM((nc, nb, quarter), F32),
            dma((7,)),
            dma((nc,)),
            dma((nb, nc)),
            dma((nc, nb)),
            dma((nb,)),
            dma((nb,)),
            dma((nc,)),
            dma((nc,)),
            dma((nb,)),
            dma((nb,)),
            dma((nc,)),
            dma((nc,)),
        ],
        compiler_params=pltpu.CompilerParams(
            collective_id=0, has_side_effects=True, vmem_limit_bytes=60 * 1024 * 1024
        ),
    )(queries, new_keys, new_values, cache_keys, cache_values, parents, lengths, out_weight)


def solution(mesh):
    placed = (
        P(("groups", "beam"), "ctx"),
        P(("groups", "beam"), None),
        P(("groups", "beam"), None),
        P(("groups", "beam"), "ctx", None, None),
        P(("groups", "beam"), "ctx", None, None),
        P("groups"),
        P("groups"),
        P("ctx", "beam"),
    )
    return jax.shard_map(
        functools.partial(per_device, mesh.shape["beam"], mesh.shape["ctx"]),
        mesh=mesh,
        in_specs=placed,
        out_specs=P("groups", ("beam", "ctx")),
        check_vma=False,
    )
```
